32 devices in a mesh: task: 4 (over y, core), fsdp: 8 (over z, x).
Axes of the slice: x: 2, y: 2, z: 4, core: 2. Of those that a mesh axis runs over, the one named last changes fastest.
Arguments:
- stitch: float32 [4, 4], replicated, may hold values from -3 to 3
- out_grad: bfloat16 [4, 4096, 1792], P('task', 'fsdp'), may hold values from -6 to 6
- block_out: bfloat16 [4, 4096, 1792], P('task', 'fsdp'), may hold values from -6 to 6
- queries: bfloat16 [4, 4096, 1792], P('task', 'fsdp'), may hold values from -80 to 80
- key_rows: bfloat16 [4, 4096, 1792], P('task', 'fsdp'), may hold values from -4 to 4
- values: bfloat16 [4, 4096, 1792], P('task', 'fsdp'), may hold values from -6 to 6
- out_proj: bfloat16 [4, 1792, 1792], P('task', 'fsdp'), may hold values from -0.125 to 0.125
Outputs:
- residual_grad: bfloat16 [4, 4096, 1792], P('task', 'fsdp')
- query_grad: bfloat16 [4, 4096, 1792], P('task', 'fsdp')
- key_grad: bfloat16 [4, 4096, 1792], P('task', 'fsdp')
- value_grad: bfloat16 [4, 4096, 1792], P('task', 'fsdp')
- proj_grad: float32 [4, 1792, 1792], P('task', 'fsdp')
- stitch_grad: float32 [4, 4], P('task')
The draws below stay inside these ranges and needn't reach their ends.
All inputs are finite; a program needn't handle non-finite values.
Results may differ from the reference program's by a relative error of at most 0.0066.
Values may be sent and summed in bfloat16 or wider, within the bound.
A program may use at most 192 MiB of HBM per device.

```python
import math
import jax
import jax.numpy as jnp
from jax import lax

D = 1792
HEADS = 16
HEAD = 112
PATCHES = 256
TASKS = 4
TOKENS = 4096


def base_rows(key):
    return jnp.clip(jax.random.normal(jax.random.fold_in(key, 11), (TASKS, TOKENS, D), jnp.float32), -4.0, 4.0)


def draw_key_rows(key, part):
    shared = base_rows(key)
    return shared.astype(jnp.bfloat16)


def draw_queries(key, part):
    key = jax.random.fold_in(key, 5)
    fresh = jnp.clip(jax.random.normal(key, (TASKS, TOKENS, D), jnp.float32), -4.0, 4.0)
    return fresh.astype(jnp.bfloat16)


def level_of(own_key, extent, split, smallest, largest):
    level, own = 1.0, jax.random.fold_in(own_key, 6)
    for position, parts in split:
        draws = jnp.exp(jax.random.uniform(jax.random.fold_in(own, position), (parts,), jnp.float32, smallest / len(split), largest / len(split)))
        level = level * jnp.repeat(draws, extent[position] // parts).reshape([-1 if axis == position else 1 for axis in range(len(extent))])
    return level


def centred(stream_key, dims, deviation, most, split=(), held_as=jnp.bfloat16):
    drawn = jax.random.normal(stream_key, dims, jnp.float32) * deviation
    if len(split) > 0:
        drawn = level_of(stream_key, dims, split, -0.22, 0.18) * drawn
    return jnp.clip(drawn, min=-most, max=most).astype(held_as)


def setup_inputs(seed: int = 0) -> dict:
    key_list = jax.random.split(jax.random.key(seed), 8)
    stitch = centred(key_list[0], (TASKS, TASKS), TASKS ** -0.5, 3.0, (), jnp.float32)
    out_grad = centred(key_list[1], (TASKS, TOKENS, D), 1.0, 6.0, ((0, 4), (1, 8)))
    block_out = centred(key_list[2], (TASKS, TOKENS, D), 1.0, 6.0, ((0, 4), (1, 8)))
    queries = draw_queries(jax.random.fold_in(key_list[7], 71), 0)
    key_rows = draw_key_rows(jax.random.fold_in(key_list[7], 71), 0)
    values = centred(key_list[5], (TASKS, TOKENS, D), 1.0, 6.0, ((0, 4), (1, 8)))
    out_proj = centred(key_list[6], (TASKS, D, D), D ** -0.5, 0.125, ((0, 4), (1, 8)))
    return dict(stitch=stitch, out_grad=out_grad, block_out=block_out, queries=queries, key_rows=key_rows, values=values, out_proj=out_proj)


def image_pair(blocks):
    query_b, key_b, value_b, upstream = blocks
    factor = 1.0 / math.sqrt(HEAD)
    scores = jnp.einsum('iphd,iqhd->ihpq', query_b.astype(jnp.float32), key_b.astype(jnp.float32)) * factor
    highest_score = lax.optimization_barrier(jnp.max(scores, axis=-1, keepdims=True))
    weights = jnp.exp(scores - highest_score)
    attn_probs = weights / lax.optimization_barrier(jnp.sum(weights, axis=-1, keepdims=True))
    probs_b = attn_probs.astype(jnp.bfloat16)
    attended = jnp.einsum('ihpq,iqhd->iphd', probs_b.astype(jnp.float32), value_b.astype(jnp.float32)).astype(jnp.bfloat16)
    dprobs = jnp.einsum('iphd,iqhd->ihpq', upstream.astype(jnp.float32), value_b.astype(jnp.float32))
    row_dots = lax.optimization_barrier(jnp.sum(attn_probs * dprobs, axis=-1, keepdims=True))
    dscores = (attn_probs * (dprobs - row_dots) * factor).astype(jnp.bfloat16)
    query_out = jnp.einsum('ihpq,iqhd->iphd', dscores.astype(jnp.float32), key_b.astype(jnp.float32)).astype(jnp.bfloat16)
    key_out = jnp.einsum('ihpq,iphd->iqhd', dscores.astype(jnp.float32), query_b.astype(jnp.float32)).astype(jnp.bfloat16)
    value_out = jnp.einsum('ihpq,iphd->iqhd', probs_b.astype(jnp.float32), upstream.astype(jnp.float32)).astype(jnp.bfloat16)
    return (attended, query_out, key_out, value_out)

def one_tower(blocks):
    mixed_rows, query_t, key_t, value_t, weight_t = blocks
    attended_grad = jnp.dot(mixed_rows, weight_t.T, preferred_element_type=jnp.float32).astype(jnp.bfloat16)

    def split_images(array):
        return array.reshape(TOKENS // (2 * PATCHES), 2, PATCHES, HEADS, HEAD)
    results = lax.map(image_pair, (split_images(query_t), split_images(key_t), split_images(value_t), split_images(attended_grad)))
    attended, query_out, key_out, value_out = [r.reshape(TOKENS, D) for r in results]
    weight_out = jnp.dot(attended.T, mixed_rows, preferred_element_type=jnp.float32)
    return (query_out, key_out, value_out, weight_out)

def reference(stitch, out_grad, block_out, queries, key_rows, values, out_proj):
    highest = lax.Precision.HIGHEST
    mixed = jnp.einsum('ts,tnd->snd', stitch, out_grad.astype(jnp.float32), precision=highest)
    residual_grad = mixed.astype(jnp.bfloat16)
    stitch_grad = jnp.einsum('tnd,snd->st', out_grad.astype(jnp.float32), block_out.astype(jnp.float32), precision=highest) / TOKENS
    query_grad, key_grad, value_grad, proj_grad = lax.map(one_tower, (residual_grad, queries, key_rows, values, out_proj))
    return (residual_grad, query_grad, key_grad, value_grad, proj_grad, stitch_grad)
```

```python
import functools
import math

import jax
import jax.numpy as jnp
from jax import lax
from jax.experimental import pallas as pl
from jax.experimental.pallas import tpu as pltpu
from jax.sharding import PartitionSpec as P

HEADS = 16
HEAD = 112
PATCHES = 256
GROUP = 8
FACTOR = 1.0 / math.sqrt(HEAD)
CORES = 2
VMEM = 40 * 1024 * 1024


def dot(a, b, ca, cb):
    return lax.dot_general(a, b, (((ca,), (cb,)), ((), ())), preferred_element_type=jnp.float32)


def softmax(q, k):
    scores = dot(q, k, 1, 1) * FACTOR
    weights = jnp.exp(scores - jnp.max(scores, axis=-1, keepdims=True))
    return weights, 1.0 / jnp.sum(weights, axis=-1, keepdims=True)


def forward_kernel(q_ref, k_ref, v_ref, o_ref):
    for head in range(GROUP):
        cols = slice(head * HEAD, (head + 1) * HEAD)
        weights, inverse = softmax(q_ref[:, cols], k_ref[:, cols])
        probs_b = (weights * inverse).astype(jnp.bfloat16)
        o_ref[:, cols] = dot(probs_b, v_ref[:, cols], 1, 0).astype(jnp.bfloat16)


def backward_kernel(q_ref, k_ref, v_ref, g_ref, dq_ref, dk_ref, dv_ref):
    for head in range(GROUP):
        cols = slice(head * HEAD, (head + 1) * HEAD)
        q, k, v, g = q_ref[:, cols], k_ref[:, cols], v_ref[:, cols], g_ref[:, cols]
        weights, inverse = softmax(q, k)
        probs = weights * inverse
        dprobs = dot(g, v, 1, 1)
        row_dots = jnp.sum(probs * dprobs, axis=-1, keepdims=True)
        dscores = (probs * (dprobs - row_dots) * FACTOR).astype(jnp.bfloat16)
        dq_ref[:, cols] = dot(dscores, k, 1, 0).astype(jnp.bfloat16)
        dk_ref[:, cols] = dot(dscores, q, 0, 0).astype(jnp.bfloat16)
        dv_ref[:, cols] = dot(probs.astype(jnp.bfloat16), g, 0, 0).astype(jnp.bfloat16)


def attention_call(kernel, outputs, matmuls, exps, *arrays):
    rows, features = arrays[0].shape
    width = GROUP * HEAD
    spec = pl.BlockSpec((PATCHES, width), lambda i, j: (i, j))
    shape = jax.ShapeDtypeStruct((rows, features), jnp.bfloat16)
    return pl.pallas_call(
        kernel,
        grid=(rows // PATCHES, features // width),
        in_specs=[spec] * len(arrays),
        out_specs=[spec] * outputs,
        out_shape=[shape] * outputs,
        compiler_params=pltpu.CompilerParams(vmem_limit_bytes=VMEM),
        cost_estimate=pl.CostEstimate(
            flops=matmuls * 2 * rows * PATCHES * features,
            bytes_accessed=2 * rows * features * (len(arrays) + outputs),
            transcendentals=rows * PATCHES * HEADS * exps,
        ),
    )(*arrays)


def stitch_kernel(towers, coef_ref, own_ref, *refs):
    pieces, (res_ref, dots_ref) = refs[:towers], refs[towers:]

    @pl.when(pl.program_id(0) == 0)
    def _():
        dots_ref[...] = jnp.zeros_like(dots_ref)

    own = own_ref[...].astype(jnp.float32)
    mixed = jnp.zeros_like(own)
    for j in range(towers):
        piece = pieces[j][...].astype(jnp.float32)
        mixed = mixed + coef_ref[0, j] * piece
        dots_ref[j : j + 1, :] += jnp.sum(piece * own, axis=0, keepdims=True)
    res_ref[...] = mixed.astype(jnp.bfloat16)


def stitch_call(coefs, own, pieces):
    rows, features = own.shape
    towers = len(pieces)
    step = 64
    spec = pl.BlockSpec((step, features), lambda i: (i, 0))
    return pl.pallas_call(
        functools.partial(stitch_kernel, towers),
        grid=(rows // step,),
        in_specs=[pl.BlockSpec(memory_space=pltpu.SMEM)] + [spec] * (towers + 1),
        out_specs=[spec, pl.BlockSpec((towers, features), lambda i: (0, 0))],
        out_shape=[
            jax.ShapeDtypeStruct((rows, features), jnp.bfloat16),
            jax.ShapeDtypeStruct((towers, features), jnp.float32),
        ],
        compiler_params=pltpu.CompilerParams(vmem_limit_bytes=VMEM),
        cost_estimate=pl.CostEstimate(
            flops=4 * rows * features * towers,
            bytes_accessed=2 * rows * features * (towers + 2),
            transcendentals=0,
        ),
    )(coefs, own, *pieces)


def tower_pieces(piece, towers, tower):
    chips = towers // CORES
    chip, core = tower // CORES, tower % CORES
    swap = [(t, t ^ 1) for t in range(towers)]
    same, owners = [piece], [tower]
    for shift in range(1, chips):
        perm = [(t, (t + CORES * shift) % towers) for t in range(towers)]
        same.append(lax.ppermute(piece, "task", perm))
        owners.append((chip - shift + chips) % chips * CORES + core)
    crossed = [lax.ppermute(block, "task", swap) for block in same]
    return same + crossed, owners + [owner + 1 - 2 * core for owner in owners]


def body(stitch, out_grad, block_out, queries, key_rows, values, out_proj):
    tower = lax.axis_index("task")
    towers = lax.axis_size("task")
    count_shards = lax.axis_size("fsdp")
    tok_rows = out_grad.shape[1]
    weight = lax.all_gather(out_proj, "fsdp", axis=1, tiled=True)[0]
    pieces, owners = tower_pieces(out_grad[0], towers, tower)
    owners = jnp.stack(owners)
    here = owners[:, None] == jnp.arange(towers)[None, :]
    column = lax.dynamic_slice_in_dim(stitch, tower, 1, 1)[:, 0]
    coefs = jnp.sum(jnp.where(here, column[None, :], 0.0), axis=1)[None, :]

    (attended,) = attention_call(forward_kernel, 1, 2, 1, queries[0], key_rows[0], values[0])
    residual, dots = stitch_call(coefs, block_out[0], pieces)
    share = lax.dot_general(
        attended, residual, (((0,), (0,)), ((), ())), preferred_element_type=jnp.float32
    ).astype(jnp.bfloat16)
    proj_grad = lax.psum_scatter(share, "fsdp", scatter_dimension=0, tiled=True)

    sums = jnp.sum(dots, axis=1)
    sums = jnp.sum(jnp.where(here, sums[:, None], 0.0), axis=0)[None, :]
    hop = 1
    while hop < count_shards:
        sums = sums + lax.ppermute(sums, "fsdp", [(d, d ^ hop) for d in range(count_shards)])
        hop *= 2
    stitch_grad = sums / (tok_rows * count_shards)

    attended_grad = lax.dot_general(
        residual, weight, (((1,), (1,)), ((), ())), preferred_element_type=jnp.float32
    ).astype(jnp.bfloat16)
    query_out, key_out, value_out = attention_call(
        backward_kernel, 3, 6, 1, queries[0], key_rows[0], values[0], attended_grad
    )
    return (
        residual[None],
        query_out[None],
        key_out[None],
        value_out[None],
        proj_grad.astype(jnp.float32)[None],
        stitch_grad,
    )


def solution(mesh):
    rows = P("task", "fsdp", None)
    return jax.shard_map(
        body,
        mesh=mesh,
        in_specs=(P(), rows, rows, rows, rows, rows, rows),
        out_specs=(rows, rows, rows, rows, rows, P("task", None)),
        check_vma=False,
    )
```

```python
import functools
import math

import jax
import jax.numpy as jnp
from jax import lax
from jax.experimental import pallas as pl
from jax.experimental.pallas import tpu as pltpu
from jax.sharding import PartitionSpec as P

HEADS = 16
HEAD = 112
PATCHES = 256
GROUP = 8
FACTOR = 1.0 / math.sqrt(HEAD)
CORES = 2
VMEM = 40 * 1024 * 1024
OUTER = 4
EARLY_X = 1152


def dot(a, b, ca, cb):
    return lax.dot_general(a, b, (((ca,), (cb,)), ((), ())), preferred_element_type=jnp.float32)


def softmax(q, k):
    scores = dot(q, k, 1, 1) * FACTOR
    weights = jnp.exp(scores - jnp.max(scores, axis=-1, keepdims=True))
    return weights, 1.0 / jnp.sum(weights, axis=-1, keepdims=True)


def forward_kernel(q_ref, k_ref, v_ref, o_ref):
    for head in range(GROUP):
        cols = slice(head * HEAD, (head + 1) * HEAD)
        weights, inverse = softmax(q_ref[:, cols], k_ref[:, cols])
        probs_b = (weights * inverse).astype(jnp.bfloat16)
        o_ref[:, cols] = dot(probs_b, v_ref[:, cols], 1, 0).astype(jnp.bfloat16)


def backward_kernel(q_ref, k_ref, v_ref, g_ref, dq_ref, dk_ref, dv_ref):
    for head in range(GROUP):
        cols = slice(head * HEAD, (head + 1) * HEAD)
        q, k, v, g = q_ref[:, cols], k_ref[:, cols], v_ref[:, cols], g_ref[:, cols]
        weights, inverse = softmax(q, k)
        probs = weights * inverse
        dprobs = dot(g, v, 1, 1)
        row_dots = jnp.sum(probs * dprobs, axis=-1, keepdims=True)
        dscores = (probs * (dprobs - row_dots) * FACTOR).astype(jnp.bfloat16)
        dq_ref[:, cols] = dot(dscores, k, 1, 0).astype(jnp.bfloat16)
        dk_ref[:, cols] = dot(dscores, q, 0, 0).astype(jnp.bfloat16)
        dv_ref[:, cols] = dot(probs.astype(jnp.bfloat16), g, 0, 0).astype(jnp.bfloat16)


def attention_call(kernel, outputs, matmuls, exps, *arrays):
    rows, features = arrays[0].shape
    width = GROUP * HEAD
    spec = pl.BlockSpec((PATCHES, width), lambda i, j: (i, j))
    shape = jax.ShapeDtypeStruct((rows, features), jnp.bfloat16)
    return pl.pallas_call(
        kernel,
        grid=(rows // PATCHES, features // width),
        in_specs=[spec] * len(arrays),
        out_specs=[spec] * outputs,
        out_shape=[shape] * outputs,
        compiler_params=pltpu.CompilerParams(vmem_limit_bytes=VMEM),
        cost_estimate=pl.CostEstimate(
            flops=matmuls * 2 * rows * PATCHES * features,
            bytes_accessed=2 * rows * features * (len(arrays) + outputs),
            transcendentals=rows * PATCHES * HEADS * exps,
        ),
    )(*arrays)


def stitch_kernel(towers, coef_ref, own_ref, *refs):
    pieces, (res_ref, dots_ref) = refs[:towers], refs[towers:]

    @pl.when(pl.program_id(0) == 0)
    def _():
        dots_ref[...] = jnp.zeros_like(dots_ref)

    own = own_ref[...].astype(jnp.float32)
    mixed = jnp.zeros_like(own)
    for j in range(towers):
        piece = pieces[j][...].astype(jnp.float32)
        mixed = mixed + coef_ref[0, j] * piece
        dots_ref[j : j + 1, :] += jnp.sum(piece * own, axis=0, keepdims=True)
    res_ref[...] = mixed.astype(jnp.bfloat16)


def stitch_call(coefs, own, pieces):
    rows, features = own.shape
    towers = len(pieces)
    step = 64
    spec = pl.BlockSpec((step, features), lambda i: (i, 0))
    return pl.pallas_call(
        functools.partial(stitch_kernel, towers),
        grid=(rows // step,),
        in_specs=[pl.BlockSpec(memory_space=pltpu.SMEM)] + [spec] * (towers + 1),
        out_specs=[spec, pl.BlockSpec((towers, features), lambda i: (0, 0))],
        out_shape=[
            jax.ShapeDtypeStruct((rows, features), jnp.bfloat16),
            jax.ShapeDtypeStruct((towers, features), jnp.float32),
        ],
        compiler_params=pltpu.CompilerParams(vmem_limit_bytes=VMEM),
        cost_estimate=pl.CostEstimate(
            flops=4 * rows * features * towers,
            bytes_accessed=2 * rows * features * (towers + 2),
            transcendentals=0,
        ),
    )(coefs, own, *pieces)


def wide(block):
    return block.astype(jnp.float32)


def sum_inner(block_for, inner, mine, shards):
    total = wide(block_for(mine))
    for shift in range(1, inner):
        perm = [(d, d // inner * inner + (d + shift) % inner) for d in range(shards)]
        total += wide(lax.ppermute(block_for((mine + shift) % inner), "fsdp", perm))
    return total


def sum_outer(block_at, inner, shards, then=None):
    right = left = None
    for far in range(OUTER - 1, 0, -1):
        ahead, behind = wide(block_at(far)), wide(block_at(OUTER - far))
        if right is not None:
            ahead, behind = ahead + wide(right), behind + wide(left)
        up = [(d, d + inner) for d in range(shards) if d // inner + far < OUTER]
        down = [(d, d - inner) for d in range(shards) if d // inner >= far]
        right = lax.ppermute(ahead.astype(jnp.bfloat16), "fsdp", up)
        left = lax.ppermute(behind.astype(jnp.bfloat16), "fsdp", down)
        if far > 1:
            right, left = lax.optimization_barrier((right, left))
        if far == 2 and then is not None:
            right, left, *then[:] = lax.optimization_barrier((right, left, *then))
    return wide(block_at(0)), right, left


def scatter_sum(share, shards, then):
    rows = share.shape[0] // shards
    inner = shards // OUTER
    place = lax.axis_index("fsdp")
    far, near = place // inner, place % inner

    def rows_of(array, start, size):
        return lax.dynamic_slice_in_dim(array, start * rows, size * rows, 0)

    first, second = share[:, :EARLY_X], share[:, EARLY_X:]
    parts = [
        sum_inner(
            lambda i, o=(far + shift) % OUTER: rows_of(first, o * inner + i, 1), inner, near, shards
        ).astype(jnp.bfloat16)
        for shift in range(OUTER)
    ]

    own, right, left = sum_outer(
        lambda shift: rows_of(second, (far + shift) % OUTER * inner, inner), inner, shards
    )
    line = (own + wide(right) + wide(left)).astype(jnp.bfloat16)
    second_sum = sum_inner(lambda i: rows_of(line, i, 1), inner, near, shards)
    return second_sum, sum_outer(lambda shift: parts[shift], inner, shards, then)


def tower_pieces(piece, towers, tower, before):
    chips = towers // CORES
    chip, core = tower // CORES, tower % CORES
    swap = [(t, t ^ 1) for t in range(towers)]
    same, owners = [piece], [tower]
    for shift in range(1, chips):
        perm = [(t, (t + CORES * shift) % towers) for t in range(towers)]
        same.append(lax.ppermute(piece, "task", perm))
        owners.append((chip - shift + chips) % chips * CORES + core)
    crossed = [lax.ppermute(piece, "task", swap)]
    moved, before = lax.optimization_barrier((same[1:], before))
    same = [piece] + moved
    crossed += [lax.ppermute(block, "task", swap) for block in moved]
    return before, same + crossed, owners + [owner + 1 - 2 * core for owner in owners]


def body(stitch, out_grad, block_out, queries, key_rows, values, out_proj):
    tower = lax.axis_index("task")
    towers = lax.axis_size("task")
    count_shards = lax.axis_size("fsdp")
    tok_rows = out_grad.shape[1]
    weight = lax.all_gather(out_proj, "fsdp", axis=1, tiled=True)[0]
    (attended,) = attention_call(forward_kernel, 1, 2, 1, queries[0], key_rows[0], values[0])
    attended, pieces, owners = tower_pieces(out_grad[0], towers, tower, attended)
    owners = jnp.stack(owners)
    here = owners[:, None] == jnp.arange(towers)[None, :]
    column = lax.dynamic_slice_in_dim(stitch, tower, 1, 1)[:, 0]
    coefs = jnp.sum(jnp.where(here, column[None, :], 0.0), axis=1)[None, :]

    residual, dots = stitch_call(coefs, block_out[0], pieces)
    share = lax.dot_general(
        attended, residual, (((0,), (0,)), ((), ())), preferred_element_type=jnp.float32
    ).astype(jnp.bfloat16)
    held = [weight]
    second_sum, (own, right, left) = scatter_sum(share, count_shards, held)
    (weight,) = held

    sums = jnp.sum(dots, axis=1)
    sums = jnp.sum(jnp.where(here, sums[:, None], 0.0), axis=0)[None, :]
    hop = 1
    while hop < count_shards:
        sums = sums + lax.ppermute(sums, "fsdp", [(d, d ^ hop) for d in range(count_shards)])
        hop *= 2
    stitch_grad = sums / (tok_rows * count_shards)

    attended_grad = lax.dot_general(
        residual, weight, (((1,), (1,)), ((), ())), preferred_element_type=jnp.float32
    ).astype(jnp.bfloat16)
    query_out, key_out, value_out = attention_call(
        backward_kernel, 3, 6, 1, queries[0], key_rows[0], values[0], attended_grad
    )
    right, left, query_out, key_out, value_out = lax.optimization_barrier(
        (right, left, query_out, key_out, value_out)
    )
    proj_grad = jnp.concatenate([own + wide(right) + wide(left), second_sum], axis=1)
    return (
        residual[None],
        query_out[None],
        key_out[None],
        value_out[None],
        proj_grad[None],
        stitch_grad,
    )


def solution(mesh):
    rows = P("task", "fsdp", None)
    return jax.shard_map(
        body,
        mesh=mesh,
        in_specs=(P(), rows, rows, rows, rows, rows, rows),
        out_specs=(rows, rows, rows, rows, rows, P("task", None)),
        check_vma=False,
    )
```

```python
import functools
import math

import jax
import jax.numpy as jnp
from jax import lax
from jax.experimental import pallas as pl
from jax.experimental.pallas import tpu as pltpu
from jax.sharding import PartitionSpec as P

HEADS = 16
HEAD = 112
PATCHES = 256
GROUP = 8
FACTOR = 1.0 / math.sqrt(HEAD)
CORES = 2
VMEM = 40 * 1024 * 1024
OUTER = 4
PERMUTED = 1280


def dot(a, b, ca, cb):
    return lax.dot_general(a, b, (((ca,), (cb,)), ((), ())), preferred_element_type=jnp.float32)


def softmax(q, k):
    scores = dot(q, k, 1, 1) * FACTOR
    weights = jnp.exp(scores - jnp.max(scores, axis=-1, keepdims=True))
    return weights, 1.0 / jnp.sum(weights, axis=-1, keepdims=True)


def forward_kernel(q_ref, k_ref, v_ref, o_ref):
    for head in range(GROUP):
        cols = slice(head * HEAD, (head + 1) * HEAD)
        weights, inverse = softmax(q_ref[:, cols], k_ref[:, cols])
        probs_b = (weights * inverse).astype(jnp.bfloat16)
        o_ref[:, cols] = dot(probs_b, v_ref[:, cols], 1, 0).astype(jnp.bfloat16)


def backward_kernel(q_ref, k_ref, v_ref, g_ref, dq_ref, dk_ref, dv_ref):
    for head in range(GROUP):
        cols = slice(head * HEAD, (head + 1) * HEAD)
        q, k, v, g = q_ref[:, cols], k_ref[:, cols], v_ref[:, cols], g_ref[:, cols]
        weights, inverse = softmax(q, k)
        probs = weights * inverse
        dprobs = dot(g, v, 1, 1)
        row_dots = jnp.sum(probs * dprobs, axis=-1, keepdims=True)
        dscores = (probs * (dprobs - row_dots) * FACTOR).astype(jnp.bfloat16)
        dq_ref[:, cols] = dot(dscores, k, 1, 0).astype(jnp.bfloat16)
        dk_ref[:, cols] = dot(dscores, q, 0, 0).astype(jnp.bfloat16)
        dv_ref[:, cols] = dot(probs.astype(jnp.bfloat16), g, 0, 0).astype(jnp.bfloat16)


def attention_call(kernel, outputs, matmuls, exps, *arrays):
    rows, features = arrays[0].shape
    width = GROUP * HEAD
    spec = pl.BlockSpec((PATCHES, width), lambda i, j: (i, j))
    shape = jax.ShapeDtypeStruct((rows, features), jnp.bfloat16)
    return pl.pallas_call(
        kernel,
        grid=(rows // PATCHES, features // width),
        in_specs=[spec] * len(arrays),
        out_specs=[spec] * outputs,
        out_shape=[shape] * outputs,
        compiler_params=pltpu.CompilerParams(vmem_limit_bytes=VMEM),
        cost_estimate=pl.CostEstimate(
            flops=matmuls * 2 * rows * PATCHES * features,
            bytes_accessed=2 * rows * features * (len(arrays) + outputs),
            transcendentals=rows * PATCHES * HEADS * exps,
        ),
    )(*arrays)


def stitch_kernel(towers, coef_ref, own_ref, *refs):
    pieces, (res_ref, dots_ref) = refs[:towers], refs[towers:]

    @pl.when(pl.program_id(0) == 0)
    def _():
        dots_ref[...] = jnp.zeros_like(dots_ref)

    own = own_ref[...].astype(jnp.float32)
    mixed = jnp.zeros_like(own)
    for j in range(towers):
        piece = pieces[j][...].astype(jnp.float32)
        mixed = mixed + coef_ref[0, j] * piece
        dots_ref[j : j + 1, :] += jnp.sum(piece * own, axis=0, keepdims=True)
    res_ref[...] = mixed.astype(jnp.bfloat16)


def stitch_call(coefs, own, pieces):
    rows, features = own.shape
    towers = len(pieces)
    step = 64
    spec = pl.BlockSpec((step, features), lambda i: (i, 0))
    return pl.pallas_call(
        functools.partial(stitch_kernel, towers),
        grid=(rows // step,),
        in_specs=[pl.BlockSpec(memory_space=pltpu.SMEM)] + [spec] * (towers + 1),
        out_specs=[spec, pl.BlockSpec((towers, features), lambda i: (0, 0))],
        out_shape=[
            jax.ShapeDtypeStruct((rows, features), jnp.bfloat16),
            jax.ShapeDtypeStruct((towers, features), jnp.float32),
        ],
        compiler_params=pltpu.CompilerParams(vmem_limit_bytes=VMEM),
        cost_estimate=pl.CostEstimate(
            flops=4 * rows * features * towers,
            bytes_accessed=2 * rows * features * (towers + 2),
            transcendentals=0,
        ),
    )(coefs, own, *pieces)


def wide(block):
    return block.astype(jnp.float32)


def sum_inner(block_for, inner, mine, shards):
    total = wide(block_for(mine))
    for shift in range(1, inner):
        perm = [(d, d // inner * inner + (d + shift) % inner) for d in range(shards)]
        total += wide(lax.ppermute(block_for((mine + shift) % inner), "fsdp", perm))
    return total


def sum_outer(block_at, inner, shards, then=None):
    right = left = None
    for far in range(OUTER - 1, 0, -1):
        ahead, behind = wide(block_at(far)), wide(block_at(OUTER - far))
        if right is not None:
            ahead, behind = ahead + wide(right), behind + wide(left)
        up = [(d, d + inner) for d in range(shards) if d // inner + far < OUTER]
        down = [(d, d - inner) for d in range(shards) if d // inner >= far]
        right = lax.ppermute(ahead.astype(jnp.bfloat16), "fsdp", up)
        left = lax.ppermute(behind.astype(jnp.bfloat16), "fsdp", down)
        if far > 1:
            right, left = lax.optimization_barrier((right, left))
        if far == 2 and then is not None:
            right, left, *then[:] = lax.optimization_barrier((right, left, *then))
    return wide(block_at(0)), right, left


def scatter_sum(share, shards, sums, then):
    rows = share.shape[0] // shards
    inner = shards // OUTER
    place = lax.axis_index("fsdp")
    far, near = place // inner, place % inner

    def block(outer, i):
        return lax.dynamic_slice_in_dim(share, (outer * inner + i) * rows, rows, 0)

    parts = [None] * OUTER
    for shift in (1, 3, 2, 0):
        outer = (far + shift) % OUTER
        parts[shift] = sum_inner(functools.partial(block, outer), inner, near, shards).astype(
            jnp.bfloat16
        )
    parts[2], sums = lax.optimization_barrier((parts[2], sums))
    return sums, sum_outer(lambda shift: parts[shift], inner, shards, then)


def tower_pieces(piece, towers, tower, before):
    chips = towers // CORES
    chip, core = tower // CORES, tower % CORES
    swap = [(t, t ^ 1) for t in range(towers)]
    same, owners = [piece], [tower]
    for shift in range(1, chips):
        perm = [(t, (t + CORES * shift) % towers) for t in range(towers)]
        same.append(lax.ppermute(piece, "task", perm))
        owners.append((chip - shift + chips) % chips * CORES + core)
    crossed = [lax.ppermute(piece, "task", swap)]
    moved, before = lax.optimization_barrier((same[1:], before))
    same = [piece] + moved
    crossed += [lax.ppermute(block, "task", swap) for block in moved]
    return before, same + crossed, owners + [owner + 1 - 2 * core for owner in owners]


def body(stitch, out_grad, block_out, queries, key_rows, values, out_proj):
    tower = lax.axis_index("task")
    towers = lax.axis_size("task")
    count_shards = lax.axis_size("fsdp")
    tok_rows = out_grad.shape[1]
    weight = lax.all_gather(out_proj, "fsdp", axis=1, tiled=True)[0]
    (attended,) = attention_call(forward_kernel, 1, 2, 1, queries[0], key_rows[0], values[0])
    attended, pieces, owners = tower_pieces(out_grad[0], towers, tower, attended)
    owners = jnp.stack(owners)
    here = owners[:, None] == jnp.arange(towers)[None, :]
    column = lax.dynamic_slice_in_dim(stitch, tower, 1, 1)[:, 0]
    coefs = jnp.sum(jnp.where(here, column[None, :], 0.0), axis=1)[None, :]

    residual, dots = stitch_call(coefs, block_out[0], pieces)
    share, rest = [
        dot(attended, part, 0, 0).astype(jnp.bfloat16)
        for part in (residual[:, :PERMUTED], residual[:, PERMUTED:])
    ]
    sums = jnp.sum(dots, axis=1)
    sums = jnp.sum(jnp.where(here, sums[:, None], 0.0), axis=0)[None, :]
    hop = 1
    while hop < count_shards:
        sums = sums + lax.ppermute(sums, "fsdp", [(d, d ^ hop) for d in range(count_shards)])
        hop *= 2
    held = [weight]
    sums, (own, right, left) = scatter_sum(share, count_shards, sums, held)
    weight, rest = lax.optimization_barrier((held[0], rest))
    rest = lax.psum_scatter(rest, "fsdp", scatter_dimension=0, tiled=True)
    stitch_grad = sums / (tok_rows * count_shards)

    attended_grad = lax.dot_general(
        residual, weight, (((1,), (1,)), ((), ())), preferred_element_type=jnp.float32
    ).astype(jnp.bfloat16)
    query_out, key_out, value_out = attention_call(
        backward_kernel, 3, 6, 1, queries[0], key_rows[0], values[0], attended_grad
    )
    right, left, query_out, key_out, value_out = lax.optimization_barrier(
        (right, left, query_out, key_out, value_out)
    )
    proj_grad = jnp.concatenate([own + wide(right) + wide(left), wide(rest)], axis=1)
    return (
        residual[None],
        query_out[None],
        key_out[None],
        value_out[None],
        proj_grad[None],
        stitch_grad,
    )


def solution(mesh):
    rows = P("task", "fsdp", None)
    return jax.shard_map(
        body,
        mesh=mesh,
        in_specs=(P(), rows, rows, rows, rows, rows, rows),
        out_specs=(rows, rows, rows, rows, rows, P("task", None)),
        check_vma=False,
    )
```

```python
import functools
import math

import jax
import jax.numpy as jnp
from jax import lax
from jax.experimental import pallas as pl
from jax.experimental.pallas import tpu as pltpu
from jax.sharding import PartitionSpec as P

HEADS = 16
HEAD = 112
PATCHES = 256
GROUP = 8
FACTOR = 1.0 / math.sqrt(HEAD)
CORES = 2
VMEM = 40 * 1024 * 1024
OUTER = 4
EARLY_X = 1152


def dot(a, b, ca, cb):
    return lax.dot_general(a, b, (((ca,), (cb,)), ((), ())), preferred_element_type=jnp.float32)


def softmax(q, k):
    scores = dot(q, k, 1, 1) * FACTOR
    weights = jnp.exp(scores - jnp.max(scores, axis=-1, keepdims=True))
    return weights, 1.0 / jnp.sum(weights, axis=-1, keepdims=True)


def forward_kernel(q_ref, k_ref, v_ref, o_ref):
    for head in range(GROUP):
        cols = slice(head * HEAD, (head + 1) * HEAD)
        weights, inverse = softmax(q_ref[:, cols], k_ref[:, cols])
        probs_b = (weights * inverse).astype(jnp.bfloat16)
        o_ref[:, cols] = dot(probs_b, v_ref[:, cols], 1, 0).astype(jnp.bfloat16)


def backward_kernel(q_ref, k_ref, v_ref, g_ref, dq_ref, dk_ref, dv_ref):
    for head in range(GROUP):
        cols = slice(head * HEAD, (head + 1) * HEAD)
        q, k, v, g = q_ref[:, cols], k_ref[:, cols], v_ref[:, cols], g_ref[:, cols]
        weights, inverse = softmax(q, k)
        probs = weights * inverse
        dprobs = dot(g, v, 1, 1)
        row_dots = jnp.sum(probs * dprobs, axis=-1, keepdims=True)
        dscores = (probs * (dprobs - row_dots) * FACTOR).astype(jnp.bfloat16)
        dq_ref[:, cols] = dot(dscores, k, 1, 0).astype(jnp.bfloat16)
        dk_ref[:, cols] = dot(dscores, q, 0, 0).astype(jnp.bfloat16)
        dv_ref[:, cols] = dot(probs.astype(jnp.bfloat16), g, 0, 0).astype(jnp.bfloat16)


def attention_call(kernel, outputs, matmuls, exps, *arrays):
    rows, features = arrays[0].shape
    width = GROUP * HEAD
    spec = pl.BlockSpec((PATCHES, width), lambda i, j: (i, j))
    shape = jax.ShapeDtypeStruct((rows, features), jnp.bfloat16)
    return pl.pallas_call(
        kernel,
        grid=(rows // PATCHES, features // width),
        in_specs=[spec] * len(arrays),
        out_specs=[spec] * outputs,
        out_shape=[shape] * outputs,
        compiler_params=pltpu.CompilerParams(vmem_limit_bytes=VMEM),
        cost_estimate=pl.CostEstimate(
            flops=matmuls * 2 * rows * PATCHES * features,
            bytes_accessed=2 * rows * features * (len(arrays) + outputs),
            transcendentals=rows * PATCHES * HEADS * exps,
        ),
    )(*arrays)


def stitch_kernel(towers, coef_ref, own_ref, *refs):
    pieces, (res_ref, dots_ref) = refs[:towers], refs[towers:]

    @pl.when(pl.program_id(0) == 0)
    def _():
        dots_ref[...] = jnp.zeros_like(dots_ref)

    own = own_ref[...].astype(jnp.float32)
    mixed = jnp.zeros_like(own)
    for j in range(towers):
        piece = pieces[j][...].astype(jnp.float32)
        mixed = mixed + coef_ref[0, j] * piece
        dots_ref[j : j + 1, :] += jnp.sum(piece * own, axis=0, keepdims=True)
    res_ref[...] = mixed.astype(jnp.bfloat16)


def stitch_call(coefs, own, pieces):
    rows, features = own.shape
    towers = len(pieces)
    step = 64
    spec = pl.BlockSpec((step, features), lambda i: (i, 0))
    return pl.pallas_call(
        functools.partial(stitch_kernel, towers),
        grid=(rows // step,),
        in_specs=[pl.BlockSpec(memory_space=pltpu.SMEM)] + [spec] * (towers + 1),
        out_specs=[spec, pl.BlockSpec((towers, features), lambda i: (0, 0))],
        out_shape=[
            jax.ShapeDtypeStruct((rows, features), jnp.bfloat16),
            jax.ShapeDtypeStruct((towers, features), jnp.float32),
        ],
        compiler_params=pltpu.CompilerParams(vmem_limit_bytes=VMEM),
        cost_estimate=pl.CostEstimate(
            flops=4 * rows * features * towers,
            bytes_accessed=2 * rows * features * (towers + 2),
            transcendentals=0,
        ),
    )(coefs, own, *pieces)


def wide(block):
    return block.astype(jnp.float32)


def sum_inner(block_for, inner, mine, shards):
    total = wide(block_for(mine))
    for shift in range(1, inner):
        perm = [(d, d // inner * inner + (d + shift) % inner) for d in range(shards)]
        total += wide(lax.ppermute(block_for((mine + shift) % inner), "fsdp", perm))
    return total


def sum_outer(block_at, inner, shards, then=None, early=None):
    right = left = None
    for far in range(OUTER - 1, 0, -1):
        ahead, behind = wide(block_at(far)), wide(block_at(OUTER - far))
        if right is not None:
            ahead, behind = ahead + wide(right), behind + wide(left)
        up = [(d, d + inner) for d in range(shards) if d // inner + far < OUTER]
        down = [(d, d - inner) for d in range(shards) if d // inner >= far]
        right = lax.ppermute(ahead.astype(jnp.bfloat16), "fsdp", up)
        left = lax.ppermute(behind.astype(jnp.bfloat16), "fsdp", down)
        if far > 1:
            right, left = lax.optimization_barrier((right, left))
        if far == OUTER - 1 and early is not None:
            right, left, *early[:] = lax.optimization_barrier((right, left, *early))
        if far == 2 and then is not None:
            right, left, *then[:] = lax.optimization_barrier((right, left, *then))
    return wide(block_at(0)), right, left


def scatter_sum(share, shards, then, early):
    rows = share.shape[0] // shards
    inner = shards // OUTER
    place = lax.axis_index("fsdp")
    far, near = place // inner, place % inner

    def rows_of(array, start, size):
        return lax.dynamic_slice_in_dim(array, start * rows, size * rows, 0)

    first, second = share[:, :EARLY_X], share[:, EARLY_X:]
    parts = [
        sum_inner(
            lambda i, o=(far + shift) % OUTER: rows_of(first, o * inner + i, 1), inner, near, shards
        ).astype(jnp.bfloat16)
        for shift in range(OUTER)
    ]

    own, right, left = sum_outer(
        lambda shift: rows_of(second, (far + shift) % OUTER * inner, inner), inner, shards, early=early
    )
    line = (own + wide(right) + wide(left)).astype(jnp.bfloat16)
    second_sum = sum_inner(lambda i: rows_of(line, i, 1), inner, near, shards)
    return second_sum, sum_outer(lambda shift: parts[shift], inner, shards, then)


def tower_pieces(piece, towers, tower, before):
    chips = towers // CORES
    chip, core = tower // CORES, tower % CORES
    swap = [(t, t ^ 1) for t in range(towers)]
    same, owners = [piece], [tower]
    for shift in range(1, chips):
        perm = [(t, (t + CORES * shift) % towers) for t in range(towers)]
        same.append(lax.ppermute(piece, "task", perm))
        owners.append((chip - shift + chips) % chips * CORES + core)
    crossed = [lax.ppermute(piece, "task", swap)]
    moved, before = lax.optimization_barrier((same[1:], before))
    same = [piece] + moved
    crossed += [lax.ppermute(block, "task", swap) for block in moved]
    return before, same + crossed, owners + [owner + 1 - 2 * core for owner in owners]


def body(stitch, out_grad, block_out, queries, key_rows, values, out_proj):
    tower = lax.axis_index("task")
    towers = lax.axis_size("task")
    count_shards = lax.axis_size("fsdp")
    tok_rows = out_grad.shape[1]
    weight = lax.all_gather(out_proj, "fsdp", axis=1, tiled=True)[0]
    (attended,) = attention_call(forward_kernel, 1, 2, 1, queries[0], key_rows[0], values[0])
    attended, pieces, owners = tower_pieces(out_grad[0], towers, tower, attended)
    owners = jnp.stack(owners)
    here = owners[:, None] == jnp.arange(towers)[None, :]
    column = lax.dynamic_slice_in_dim(stitch, tower, 1, 1)[:, 0]
    coefs = jnp.sum(jnp.where(here, column[None, :], 0.0), axis=1)[None, :]

    residual, dots = stitch_call(coefs, block_out[0], pieces)
    share = lax.dot_general(
        attended, residual, (((0,), (0,)), ((), ())), preferred_element_type=jnp.float32
    ).astype(jnp.bfloat16)
    sums = jnp.sum(dots, axis=1)
    sums = jnp.sum(jnp.where(here, sums[:, None], 0.0), axis=0)[None, :]
    hop = 1
    while hop < count_shards:
        sums = sums + lax.ppermute(sums, "fsdp", [(d, d ^ hop) for d in range(count_shards)])
        hop *= 2
    held, early = [weight], [sums]
    second_sum, (own, right, left) = scatter_sum(share, count_shards, held, early)
    (weight,) = held

    stitch_grad = early[0] / (tok_rows * count_shards)

    attended_grad = lax.dot_general(
        residual, weight, (((1,), (1,)), ((), ())), preferred_element_type=jnp.float32
    ).astype(jnp.bfloat16)
    query_out, key_out, value_out = attention_call(
        backward_kernel, 3, 6, 1, queries[0], key_rows[0], values[0], attended_grad
    )
    right, left, query_out, key_out, value_out = lax.optimization_barrier(
        (right, left, query_out, key_out, value_out)
    )
    proj_grad = jnp.concatenate([own + wide(right) + wide(left), second_sum], axis=1)
    return (
        residual[None],
        query_out[None],
        key_out[None],
        value_out[None],
        proj_grad[None],
        stitch_grad,
    )


def solution(mesh):
    rows = P("task", "fsdp", None)
    return jax.shard_map(
        body,
        mesh=mesh,
        in_specs=(P(), rows, rows, rows, rows, rows, rows),
        out_specs=(rows, rows, rows, rows, rows, P("task", None)),
        check_vma=False,
    )
```
